32 devices in a mesh: expert: 8 (over y, x, core), dp: 4 (over z).
Axes of the slice: x: 2, y: 2, z: 4, core: 2. Of those that a mesh axis runs over, the one named last changes fastest.
Arguments:
- tokens: bfloat16 [4096, 2048], P(('expert', 'dp')), may hold values from -6 to 6
- cotangent: bfloat16 [4096, 2048], P(('expert', 'dp')), may hold values from -6 to 6
- expert_ids: int32 [4096, 8], P(('expert', 'dp')), may hold values from 0 to 63, as said below
- gate_weights: float32 [4096, 8], P(('expert', 'dp')), may hold values from 0.05 to 1
- placement: int32 [8], replicated, may hold values from 0 to 7, as said below
- w_in: bfloat16 [8, 2048, 1536], P('expert'), may hold values from -0.125 to 0.125
- w_out: bfloat16 [8, 768, 2048], P('expert'), may hold values from -0.21875 to 0.21875
Outputs:
- mixed: bfloat16 [4096, 2048], P(('expert', 'dp'))
- x_grad: bfloat16 [4096, 2048], P(('expert', 'dp'))
- gate_grad: float32 [4096, 8], P(('expert', 'dp'))
- w_in_grad: bfloat16 [8, 2048, 1536], P('expert', 'dp')
- w_out_grad: bfloat16 [8, 768, 2048], P('expert', 'dp')
The draws below stay inside these ranges and needn't reach their ends.
Inputs may be any that keep to these rules, and one draw needn't show every extreme that they name: `expert_ids`: each row names 8 different experts, at most two of them below 8. Among the 128 tokens of one device (an aligned block of rows, one data group every 4 blocks), no expert below 8 is named by more than 16 tokens, and in every data group one such expert is named by exactly 16 tokens of every device of the group. placement[i] is i or (i + 4) % 8, and placement[placement[i]] = i; at least one pair exchanges and at least one pair stays.
All inputs are finite; a program needn't handle non-finite values.
Results may differ from the reference program's by a relative error of at most 0.018.
Values may be sent and summed in bfloat16 or wider, within the bound.
A program may use at most 128 MiB of HBM per device.

```python
import math
import jax
import jax.numpy as jnp
from jax import lax

D = 2048
FF = 768
TOP = 8
TOK_DEV = 128
CAP = 16
EXPERTS = 8
ROUTED = 64
GROUPS = 4
TOKENS = 4096


def draw_expert_ids(key, part):
    blocks = TOKENS // TOK_DEV
    group_count = blocks // EXPERTS
    key_level, key_full, key_count, key_order, key_offset, key_turn = jax.random.split(key, 6)
    level = jax.random.randint(key_level, (group_count, EXPERTS), CAP // 2, CAP + 1)
    full_expert = jax.random.randint(key_full, (group_count,), 0, EXPERTS)
    block_group = jnp.arange(blocks, dtype=jnp.int32) % group_count
    raw_count = jax.random.randint(key_count, (blocks, EXPERTS), 0, 1 << 20)
    block_level = level[block_group]
    counts = block_level - raw_count % (block_level // 2 + 1)
    expert_lane = jnp.arange(EXPERTS, dtype=jnp.int32)
    counts = jnp.where(expert_lane[None, :] == full_expert[block_group][:, None], CAP, counts)
    starts = jnp.cumsum(counts, axis=1) - counts
    order_keys = jax.random.split(key_order, blocks)
    order = jax.vmap(lambda subkey: jax.random.permutation(subkey, TOK_DEV))(order_keys).astype(jnp.int32)
    covered = (order[:, :, None] - starts[:, None, :]) % TOK_DEV < counts[:, None, :]
    covered = covered.reshape(TOKENS, EXPERTS)
    cover_count = jnp.sum(covered.astype(jnp.int32), axis=1)
    first_pick = jnp.argmax(covered, axis=1).astype(jnp.int32)
    last_pick = (EXPERTS - 1 - jnp.argmax(covered[:, ::-1], axis=1)).astype(jnp.int32)
    offset = jax.random.randint(key_offset, (TOKENS,), 0, ROUTED - EXPERTS)
    turn = jax.random.randint(key_turn, (TOKENS,), 0, TOP)
    slot_lane = jnp.arange(TOP, dtype=jnp.int32)
    outside = EXPERTS + (offset[:, None] + slot_lane[None, :]) % (ROUTED - EXPERTS)
    listed = jnp.where((slot_lane[None, :] == 0) & (cover_count[:, None] >= 1), first_pick[:, None], outside)
    listed = jnp.where((slot_lane[None, :] == 1) & (cover_count[:, None] >= 2), last_pick[:, None], listed)
    rolled = ((slot_lane[None, :] + turn[:, None]) % TOP).astype(jnp.int32)
    return jnp.take_along_axis(listed, rolled, axis=1).astype(jnp.int32)


def draw_placement(key, part):
    half_count = EXPERTS // 2
    key_flag, key_first, key_second = jax.random.split(key, 3)
    flags = jax.random.randint(key_flag, (half_count,), 0, 2)
    first_pair = jax.random.randint(key_first, (), 0, half_count)
    second_pair = (first_pair + jax.random.randint(key_second, (), 1, half_count)) % half_count
    pair_lane = jnp.arange(half_count, dtype=jnp.int32)
    flags = jnp.where(pair_lane == first_pair, 1, jnp.where(pair_lane == second_pair, 0, flags))
    return jnp.concatenate([pair_lane + half_count * flags, pair_lane + half_count * (1 - flags)]).astype(jnp.int32)


def levels(stream_key, dims, cuts, low, high):
    factor_of, own = 1.0, jax.random.fold_in(stream_key, 6)
    for dim, parts in cuts:
        draws = jnp.exp(jax.random.uniform(jax.random.fold_in(own, dim), (parts,), jnp.float32, low / len(cuts), high / len(cuts)))
        factor_of = factor_of * jnp.repeat(draws, dims[dim] // parts).reshape([-1 if axis == dim else 1 for axis in range(len(dims))])
    return factor_of


def bell_draw(key, dims, spread, limit, pieces=(), held_as=jnp.bfloat16):
    level = levels(key, dims, pieces, -0.22, 0.18) if pieces else 1.0
    result = jax.random.normal(key, dims, jnp.float32) * spread * level
    return jnp.minimum(jnp.maximum(result, -limit), limit).astype(held_as)


def setup_inputs(seed: int = 0) -> dict:
    splits = jax.random.split(jax.random.key(seed), 8)
    tokens = bell_draw(splits[0], (TOKENS, D), 1.0, 6.0, ((0, 32),))
    cotangent = bell_draw(splits[1], (TOKENS, D), 1.0, 6.0, ((0, 32),))
    expert_ids = draw_expert_ids(jax.random.fold_in(splits[7], 71), 0)
    gate_weights = jnp.clip(jnp.exp(math.log(1.0) - 2.9957323 * jax.random.uniform(splits[3], (TOKENS, TOP), jnp.float32) ** levels(splits[3], (TOKENS, TOP), ((0, 32),), -0.2, 0.2)), 0.05, 1.0)
    placement = draw_placement(jax.random.fold_in(splits[7], 71), 0)
    w_in = bell_draw(splits[5], (EXPERTS, D, 2 * FF), D ** -0.5, 0.125, ((0, 8),))
    w_out = bell_draw(splits[6], (EXPERTS, FF, D), FF ** -0.5, 0.21875, ((0, 8),))
    return {"tokens": tokens, "cotangent": cotangent, "expert_ids": expert_ids, "gate_weights": gate_weights, "placement": placement, "w_in": w_in, "w_out": w_out}


def reference(tokens, cotangent, expert_ids, gate_weights, placement, w_in, w_out):
    highest = lax.Precision.HIGHEST
    position = jnp.arange(TOKENS, dtype=jnp.int32)
    group_of = (position // TOK_DEV) % GROUPS
    group_lane = jnp.arange(GROUPS, dtype=jnp.int32)
    row_limit = EXPERTS * CAP

    def one_expert(carry, expert):
        mixed_sum, grad_sum, gate_sum = carry
        is_hit = expert_ids == expert
        chosen = jnp.any(is_hit, axis=1)
        gate_value = jnp.sum(jnp.where(is_hit, gate_weights, 0.0), axis=1)
        sort_keys = jnp.where(chosen[None, :] & (group_of[None, :] == group_lane[:, None]), position[None, :], TOKENS)
        sort_keys = jnp.sort(sort_keys, axis=1)[:, :row_limit].astype(jnp.int32)
        is_valid = sort_keys < TOKENS
        row_index = jnp.minimum(sort_keys, TOKENS - 1).astype(jnp.int32)
        picked_x = jnp.where(is_valid[..., None], tokens[row_index], jnp.zeros((), tokens.dtype))
        weight_in = lax.dynamic_index_in_dim(w_in, expert, 0, keepdims=False).astype(jnp.float32)
        weight_out = lax.dynamic_index_in_dim(w_out, expert, 0, keepdims=False).astype(jnp.float32)
        pre = jnp.einsum("gmd,df->gmf", picked_x.astype(jnp.float32), weight_in, precision=highest)
        gate_pre = pre[..., :FF]
        up_pre = pre[..., FF:]
        sigmoid_gate = jax.nn.sigmoid(gate_pre)
        activated = gate_pre * sigmoid_gate
        hidden = (activated * up_pre).astype(jnp.bfloat16)
        expert_out = jnp.einsum("gmf,fd->gmd", hidden.astype(jnp.float32), weight_out, precision=highest).astype(jnp.bfloat16)
        pick_gate = jnp.where(is_valid, gate_value[row_index], 0.0)
        picked_dy = cotangent[row_index].astype(jnp.float32)
        scaled = (picked_dy * pick_gate[..., None]).astype(jnp.bfloat16)
        hidden_grad = jnp.einsum("gmd,fd->gmf", scaled.astype(jnp.float32), weight_out, precision=highest)
        gate_up_grad = jnp.concatenate(
            [hidden_grad * up_pre * sigmoid_gate * (1.0 + gate_pre * (1.0 - sigmoid_gate)), hidden_grad * activated],
            axis=-1).astype(jnp.bfloat16)
        pick_grad = jnp.einsum("gmf,df->gmd", gate_up_grad.astype(jnp.float32), weight_in, precision=highest).astype(jnp.bfloat16)
        partial_in = jnp.einsum("gmd,gmf->gdf", picked_x.astype(jnp.float32), gate_up_grad.astype(jnp.float32), precision=highest).astype(jnp.bfloat16)
        partial_out = jnp.einsum("gmf,gmd->gfd", hidden.astype(jnp.float32), scaled.astype(jnp.float32), precision=highest).astype(jnp.bfloat16)
        grad_in = (jnp.sum(partial_in.astype(jnp.float32), axis=0) / GROUPS).astype(jnp.bfloat16)
        grad_out = (jnp.sum(partial_out.astype(jnp.float32), axis=0) / GROUPS).astype(jnp.bfloat16)
        flat_index = row_index.reshape(-1)
        flat_valid = is_valid.reshape(-1)
        contribution = (pick_gate[..., None] * expert_out.astype(jnp.float32)).reshape(-1, D)
        mixed_sum = mixed_sum.at[flat_index].add(jnp.where(flat_valid[:, None], contribution, 0.0))
        grad_sum = grad_sum.at[flat_index].add(jnp.where(flat_valid[:, None], pick_grad.astype(jnp.float32).reshape(-1, D), 0.0))
        score = jnp.sum(picked_dy * expert_out.astype(jnp.float32), axis=-1).reshape(-1)
        token_score = jnp.zeros((TOKENS,), jnp.float32).at[flat_index].add(jnp.where(flat_valid, score, 0.0))
        gate_sum = gate_sum + jnp.where(is_hit, token_score[:, None], 0.0)
        return (mixed_sum, grad_sum, gate_sum), (grad_in, grad_out)

    start = (jnp.zeros((TOKENS, D), jnp.float32), jnp.zeros((TOKENS, D), jnp.float32), jnp.zeros((TOKENS, TOP), jnp.float32))
    final, stacked = lax.scan(one_expert, start, jnp.arange(EXPERTS, dtype=jnp.int32))
    mixed_sum, grad_sum, gate_sum = final
    grads_in, grads_out = stacked
    return (mixed_sum.astype(jnp.bfloat16), grad_sum.astype(jnp.bfloat16), gate_sum,
            jnp.take(grads_in, placement, axis=0), jnp.take(grads_out, placement, axis=0))
```

```python
import jax
import jax.numpy as jnp
from jax import lax
from jax.sharding import PartitionSpec as P

F32 = jnp.float32
BF16 = jnp.bfloat16


def hidden_parts(rows_x, weight_in, hidden_units):
    pre = jnp.dot(rows_x, weight_in, preferred_element_type=F32)
    gate_pre = pre[:, :hidden_units]
    up_pre = pre[:, hidden_units:]
    sigmoid_gate = jax.nn.sigmoid(gate_pre)
    activated = gate_pre * sigmoid_gate
    hidden = (activated * up_pre).astype(BF16)
    slope = up_pre * sigmoid_gate * (1.0 + gate_pre * (1.0 - sigmoid_gate))
    return hidden, activated, slope


def pre_grad(rows_c, weight_out, activated, slope):
    hidden_grad = jnp.einsum("sd,fd->sf", rows_c, weight_out, preferred_element_type=F32)
    return jnp.concatenate([hidden_grad * slope, hidden_grad * activated], axis=1).astype(BF16)


def shards(tokens, cotangent, expert_ids, gate_weights, placement, w_in, w_out):
    expert_count = lax.axis_size("expert")
    group_count = lax.axis_size("dp")
    own_index = lax.axis_index("expert")
    group = lax.axis_index("dp")
    tok_rows, model_width = tokens.shape
    hidden_units = w_out.shape[1]
    capacity = tok_rows // 8
    slot_count = expert_count * capacity
    expert_lane = jnp.arange(expert_count, dtype=jnp.int32)
    placed_here = jnp.sum(jnp.where(expert_lane == own_index, placement, 0))
    is_moved = placed_here != own_index
    weight_in, weight_out = w_in[0], w_out[0]

    pick_hot = expert_ids[:, :, None] == expert_lane[None, None, :]
    expert_hot = jnp.any(pick_hot, axis=1)
    gate_of = jnp.sum(jnp.where(pick_hot, gate_weights[:, :, None], 0.0), axis=1)
    row = jnp.arange(tok_rows, dtype=jnp.int32)
    below = (row[None, :] < row[:, None]).astype(BF16)
    rank = jnp.dot(below, expert_hot.astype(BF16), preferred_element_type=F32).astype(jnp.int32)
    rank = jnp.where(expert_hot, rank, -1)
    slot_hot = rank[:, :, None] == jnp.arange(capacity, dtype=jnp.int32)[None, None, :]
    select = slot_hot.astype(BF16).reshape(tok_rows, slot_count)
    weigh = jnp.where(slot_hot, gate_of[:, :, None], 0.0).reshape(tok_rows, slot_count)
    slot_gate = jnp.sum(weigh, axis=0)

    send_x = jnp.einsum("ts,td->sd", select, tokens, preferred_element_type=F32).astype(BF16)
    send_dy = jnp.einsum("ts,td->sd", select, cotangent, preferred_element_type=F32)
    send_c = (send_dy * slot_gate[:, None]).astype(BF16)
    send = jnp.stack([send_x, send_c], axis=0).reshape(2, expert_count, capacity, model_width)
    arrived = lax.all_to_all(send, "expert", split_axis=1, concat_axis=1, tiled=True)
    arrived = arrived.reshape(2, slot_count, model_width)

    gathered = lax.all_gather(arrived, "dp", axis=1, tiled=True)

    hidden, activated, slope = hidden_parts(arrived[0], weight_in, hidden_units)
    expert_out = jnp.dot(hidden, weight_out, preferred_element_type=F32).astype(BF16)
    gate_up_grad = pre_grad(arrived[1], weight_out, activated, slope)
    pick_grad = jnp.einsum("sf,df->sd", gate_up_grad, weight_in, preferred_element_type=F32)
    back = jnp.stack([expert_out, pick_grad.astype(BF16)], axis=0)
    back = back.reshape(2, expert_count, capacity, model_width)
    back = lax.all_to_all(back, "expert", split_axis=1, concat_axis=1, tiled=True)
    back = back.reshape(2, slot_count, model_width)
    returned, back_grad = back[0], back[1]

    all_x, all_c = gathered[0], gathered[1]
    hidden, activated, slope = hidden_parts(all_x, weight_in, hidden_units)
    in_rows = model_width // group_count
    out_rows = hidden_units // group_count
    hidden_part = lax.dynamic_slice_in_dim(hidden, group * out_rows, out_rows, axis=1)
    grad_out = jnp.einsum("sf,sd->fd", hidden_part, all_c, preferred_element_type=F32)
    grad_out = (grad_out / group_count).astype(BF16)
    gate_up_grad = pre_grad(all_c, weight_out, activated, slope)
    x_part = lax.dynamic_slice_in_dim(all_x, group * in_rows, in_rows, axis=1)
    grad_in = jnp.einsum("sd,sf->df", x_part, gate_up_grad, preferred_element_type=F32)
    grad_in = (grad_in / group_count).astype(BF16)
    half = expert_count // 2
    route = [(i, (i + half) % expert_count) for i in range(expert_count)]
    swapped_out = lax.ppermute(grad_out, "expert", route)
    swapped_in = lax.ppermute(grad_in, "expert", route)

    weigh_high = weigh.astype(BF16)
    rest = weigh - weigh_high.astype(F32)
    weigh_mid = rest.astype(BF16)
    weigh_low = (rest - weigh_mid.astype(F32)).astype(BF16)
    mixed = jnp.dot(weigh_high, returned, preferred_element_type=F32)
    mixed += jnp.dot(weigh_mid, returned, preferred_element_type=F32)
    mixed += jnp.dot(weigh_low, returned, preferred_element_type=F32)
    scores = jnp.einsum("td,sd->ts", cotangent, returned, preferred_element_type=F32)
    scores = scores.reshape(tok_rows, expert_count, capacity)
    score_of = jnp.sum(jnp.where(slot_hot, scores, 0.0), axis=2)
    gate_grad = jnp.sum(jnp.where(pick_hot, score_of[:, None, :], 0.0), axis=2)
    x_grad = jnp.dot(select, back_grad, preferred_element_type=F32)
    grad_in = jnp.where(is_moved, swapped_in, grad_in)
    grad_out = jnp.where(is_moved, swapped_out, grad_out)
    return (mixed.astype(BF16), x_grad.astype(BF16), gate_grad, grad_in[None], grad_out[None])


def solution(mesh):
    rows = P(("expert", "dp"), None)
    weights = P("expert", None, None)
    grads = P("expert", "dp", None)
    return jax.shard_map(
        shards,
        mesh=mesh,
        in_specs=(rows, rows, rows, rows, P(), weights, weights),
        out_specs=(rows, rows, rows, grads, grads),
        check_vma=False,
    )
```

```python
import jax
import jax.numpy as jnp
from jax import lax
from jax.sharding import PartitionSpec as P

F32 = jnp.float32
BF16 = jnp.bfloat16


def hidden_parts(rows_x, weight_in, hidden_units):
    pre = jnp.dot(rows_x, weight_in, preferred_element_type=F32)
    gate_pre = pre[:, :hidden_units]
    up_pre = pre[:, hidden_units:]
    sigmoid_gate = jax.nn.sigmoid(gate_pre)
    activated = gate_pre * sigmoid_gate
    hidden = (activated * up_pre).astype(BF16)
    slope = up_pre * sigmoid_gate * (1.0 + gate_pre * (1.0 - sigmoid_gate))
    return hidden, activated, slope


def pre_grad(rows_c, weight_out, activated, slope):
    hidden_grad = jnp.einsum("sd,fd->sf", rows_c, weight_out, preferred_element_type=F32)
    return jnp.concatenate([hidden_grad * slope, hidden_grad * activated], axis=1).astype(BF16)


def exchange_columns(block, group, group_count):
    rows, width = block.shape
    part = width // group_count
    whole = jnp.zeros((group_count, rows, part), block.dtype)
    for shift in range(group_count):
        target = (group + shift) % group_count
        source = (group + group_count - shift) % group_count
        piece = lax.dynamic_slice_in_dim(block, target * part, part, axis=1)
        if shift:
            piece = lax.ppermute(piece, "dp", [(i, (i + shift) % group_count) for i in range(group_count)])
        whole = lax.dynamic_update_index_in_dim(whole, piece, source, axis=0)
    return whole.reshape(group_count * rows, part)


def shards(tokens, cotangent, expert_ids, gate_weights, placement, w_in, w_out):
    expert_count = lax.axis_size("expert")
    group_count = lax.axis_size("dp")
    own_index = lax.axis_index("expert")
    group = lax.axis_index("dp")
    tok_rows, model_width = tokens.shape
    hidden_units = w_out.shape[1]
    capacity = tok_rows // 8
    slot_count = expert_count * capacity
    expert_lane = jnp.arange(expert_count, dtype=jnp.int32)
    placed_here = jnp.sum(jnp.where(expert_lane == own_index, placement, 0))
    is_moved = placed_here != own_index
    weight_in, weight_out = w_in[0], w_out[0]

    pick_hot = expert_ids[:, :, None] == expert_lane[None, None, :]
    expert_hot = jnp.any(pick_hot, axis=1)
    gate_of = jnp.sum(jnp.where(pick_hot, gate_weights[:, :, None], 0.0), axis=1)
    row = jnp.arange(tok_rows, dtype=jnp.int32)
    below = (row[None, :] < row[:, None]).astype(BF16)
    rank = jnp.dot(below, expert_hot.astype(BF16), preferred_element_type=F32).astype(jnp.int32)
    rank = jnp.where(expert_hot, rank, -1)
    slot_hot = rank[:, :, None] == jnp.arange(capacity, dtype=jnp.int32)[None, None, :]
    select = slot_hot.astype(BF16).reshape(tok_rows, slot_count)
    weigh = jnp.where(slot_hot, gate_of[:, :, None], 0.0).reshape(tok_rows, slot_count)
    slot_gate = jnp.sum(weigh, axis=0)

    send_x = jnp.einsum("ts,td->sd", select, tokens, preferred_element_type=F32).astype(BF16)
    send_dy = jnp.einsum("ts,td->sd", select, cotangent, preferred_element_type=F32)
    send_c = (send_dy * slot_gate[:, None]).astype(BF16)
    send = jnp.stack([send_x, send_c], axis=0).reshape(2, expert_count, capacity, model_width)
    arrived = lax.all_to_all(send, "expert", split_axis=1, concat_axis=1, tiled=True)
    arrived = arrived.reshape(2, slot_count, model_width)

    hidden, activated, slope = hidden_parts(arrived[0], weight_in, hidden_units)
    gate_up_grad = pre_grad(arrived[1], weight_out, activated, slope)
    x_slices = exchange_columns(arrived[0], group, group_count)
    all_grad = lax.all_gather(gate_up_grad, "dp", axis=0, tiled=True)
    hidden_slices = exchange_columns(hidden, group, group_count)
    expert_out = jnp.dot(hidden, weight_out, preferred_element_type=F32).astype(BF16)
    pick_grad = jnp.einsum("sf,df->sd", gate_up_grad, weight_in, preferred_element_type=F32)
    back = jnp.stack([expert_out, pick_grad.astype(BF16)], axis=0)
    back = back.reshape(2, expert_count, capacity, model_width)
    back = lax.all_to_all(back, "expert", split_axis=1, concat_axis=1, tiled=True)
    back = back.reshape(2, slot_count, model_width)
    returned, back_grad = back[0], back[1]

    half = expert_count // 2
    route = [(i, (i + half) % expert_count) for i in range(expert_count)]
    own_c, all_grad = lax.optimization_barrier((arrived[1], all_grad))
    all_c = lax.all_gather(own_c, "dp", axis=0, tiled=True)
    grad_in = jnp.einsum("sd,sf->df", x_slices, all_grad, preferred_element_type=F32)
    grad_in = (grad_in / group_count).astype(BF16)
    swapped_in = lax.ppermute(grad_in, "expert", route)
    grad_out = jnp.einsum("sf,sd->fd", hidden_slices, all_c, preferred_element_type=F32)
    grad_out = (grad_out / group_count).astype(BF16)
    swapped_out = lax.ppermute(grad_out, "expert", route)

    weigh_high = weigh.astype(BF16)
    rest = weigh - weigh_high.astype(F32)
    weigh_mid = rest.astype(BF16)
    weigh_low = (rest - weigh_mid.astype(F32)).astype(BF16)
    mixed = jnp.dot(weigh_high, returned, preferred_element_type=F32)
    mixed += jnp.dot(weigh_mid, returned, preferred_element_type=F32)
    mixed += jnp.dot(weigh_low, returned, preferred_element_type=F32)
    scores = jnp.einsum("td,sd->ts", cotangent, returned, preferred_element_type=F32)
    scores = scores.reshape(tok_rows, expert_count, capacity)
    score_of = jnp.sum(jnp.where(slot_hot, scores, 0.0), axis=2)
    gate_grad = jnp.sum(jnp.where(pick_hot, score_of[:, None, :], 0.0), axis=2)
    x_grad = jnp.dot(select, back_grad, preferred_element_type=F32)
    grad_in = jnp.where(is_moved, swapped_in, grad_in)
    grad_out = jnp.where(is_moved, swapped_out, grad_out)
    return (mixed.astype(BF16), x_grad.astype(BF16), gate_grad, grad_in[None], grad_out[None])


def solution(mesh):
    rows = P(("expert", "dp"), None)
    weights = P("expert", None, None)
    grads = P("expert", "dp", None)
    return jax.shard_map(
        shards,
        mesh=mesh,
        in_specs=(rows, rows, rows, rows, P(), weights, weights),
        out_specs=(rows, rows, rows, grads, grads),
        check_vma=False,
    )
```

```python
import jax
import jax.numpy as jnp
from jax import lax
from jax.sharding import PartitionSpec as P

F32 = jnp.float32
BF16 = jnp.bfloat16


def hidden_parts(rows_x, weight_in, hidden_units):
    pre = jnp.dot(rows_x, weight_in, preferred_element_type=F32)
    gate_pre = pre[:, :hidden_units]
    up_pre = pre[:, hidden_units:]
    sigmoid_gate = jax.nn.sigmoid(gate_pre)
    activated = gate_pre * sigmoid_gate
    hidden = (activated * up_pre).astype(BF16)
    slope = up_pre * sigmoid_gate * (1.0 + gate_pre * (1.0 - sigmoid_gate))
    return hidden, activated, slope


def pre_grad(rows_c, weight_out, activated, slope):
    hidden_grad = jnp.einsum("sd,fd->sf", rows_c, weight_out, preferred_element_type=F32)
    return jnp.concatenate([hidden_grad * slope, hidden_grad * activated], axis=1).astype(BF16)


def exchange_columns(block, group, group_count):
    rows, width = block.shape
    part = width // group_count
    whole = jnp.zeros((group_count, rows, part), block.dtype)
    for shift in range(group_count):
        target = (group + shift) % group_count
        source = (group + group_count - shift) % group_count
        piece = lax.dynamic_slice_in_dim(block, target * part, part, axis=1)
        if shift:
            piece = lax.ppermute(piece, "dp", [(i, (i + shift) % group_count) for i in range(group_count)])
        whole = lax.dynamic_update_index_in_dim(whole, piece, source, axis=0)
    return whole.reshape(group_count * rows, part)


def shards(tokens, cotangent, expert_ids, gate_weights, placement, w_in, w_out):
    expert_count = lax.axis_size("expert")
    group_count = lax.axis_size("dp")
    own_index = lax.axis_index("expert")
    group = lax.axis_index("dp")
    tok_rows, model_width = tokens.shape
    hidden_units = w_out.shape[1]
    capacity = tok_rows // 8
    slot_count = expert_count * capacity
    expert_lane = jnp.arange(expert_count, dtype=jnp.int32)
    placed_here = jnp.sum(jnp.where(expert_lane == own_index, placement, 0))
    is_moved = placed_here != own_index
    weight_in, weight_out = w_in[0], w_out[0]

    pick_hot = expert_ids[:, :, None] == expert_lane[None, None, :]
    expert_hot = jnp.any(pick_hot, axis=1)
    gate_of = jnp.sum(jnp.where(pick_hot, gate_weights[:, :, None], 0.0), axis=1)
    row = jnp.arange(tok_rows, dtype=jnp.int32)
    below = (row[None, :] < row[:, None]).astype(BF16)
    rank = jnp.dot(below, expert_hot.astype(BF16), preferred_element_type=F32).astype(jnp.int32)
    rank = jnp.where(expert_hot, rank, -1)
    slot_hot = rank[:, :, None] == jnp.arange(capacity, dtype=jnp.int32)[None, None, :]
    select = slot_hot.astype(BF16).reshape(tok_rows, slot_count)
    weigh = jnp.where(slot_hot, gate_of[:, :, None], 0.0).reshape(tok_rows, slot_count)
    slot_gate = jnp.sum(weigh, axis=0)

    send_x = jnp.einsum("ts,td->sd", select, tokens, preferred_element_type=F32).astype(BF16)
    send_dy = jnp.einsum("ts,td->sd", select, cotangent, preferred_element_type=F32)
    send_c = (send_dy * slot_gate[:, None]).astype(BF16)
    send = jnp.stack([send_x, send_c], axis=0).reshape(2, expert_count, capacity, model_width)
    arrived = lax.all_to_all(send, "expert", split_axis=1, concat_axis=1, tiled=True)
    arrived = arrived.reshape(2, slot_count, model_width)

    hidden, activated, slope = hidden_parts(arrived[0], weight_in, hidden_units)
    gate_up_grad = pre_grad(arrived[1], weight_out, activated, slope)
    x_slices = exchange_columns(arrived[0], group, group_count)
    all_grad = lax.all_gather(gate_up_grad, "dp", axis=0, tiled=True)
    expert_out = jnp.dot(hidden, weight_out, preferred_element_type=F32).astype(BF16)
    pick_grad = jnp.einsum("sf,df->sd", gate_up_grad, weight_in, preferred_element_type=F32)
    back = jnp.stack([expert_out, pick_grad.astype(BF16)], axis=0)
    back = back.reshape(2, expert_count, capacity, model_width)
    back, x_slices = lax.optimization_barrier((back, x_slices))
    back = lax.all_to_all(back, "expert", split_axis=1, concat_axis=1, tiled=True)
    back = back.reshape(2, slot_count, model_width)
    returned, back_grad = back[0], back[1]

    half = expert_count // 2
    route = [(i, (i + half) % expert_count) for i in range(expert_count)]
    middle = model_width // 2
    first_c, all_grad = lax.optimization_barrier((arrived[1][:, :middle], all_grad))
    all_c1 = lax.all_gather(first_c, "dp", axis=0, tiled=True)
    grad_in = jnp.einsum("sd,sf->df", x_slices, all_grad, preferred_element_type=F32)
    grad_in = (grad_in / group_count).astype(BF16)
    own_hidden, grad_in = lax.optimization_barrier((hidden, grad_in))
    hidden_slices = exchange_columns(own_hidden, group, group_count)
    half_rows = grad_in.shape[0] // 2
    swapped_top = lax.ppermute(grad_in[:half_rows], "expert", route)
    swapped_low = lax.ppermute(grad_in[half_rows:], "expert", route)
    second_c, hidden_slices, all_c1, swapped_top = lax.optimization_barrier(
        (arrived[1][:, middle:], hidden_slices, all_c1, swapped_top)
    )
    all_c2 = lax.all_gather(second_c, "dp", axis=0, tiled=True)
    outs = []
    for all_c in (all_c1, all_c2):
        grad_out = jnp.einsum("sf,sd->fd", hidden_slices, all_c, preferred_element_type=F32)
        grad_out = (grad_out / group_count).astype(BF16)
        outs.append((grad_out, lax.ppermute(grad_out, "expert", route)))

    weigh_high = weigh.astype(BF16)
    rest = weigh - weigh_high.astype(F32)
    weigh_mid = rest.astype(BF16)
    weigh_low = (rest - weigh_mid.astype(F32)).astype(BF16)
    mixed = jnp.dot(weigh_high, returned, preferred_element_type=F32)
    mixed += jnp.dot(weigh_mid, returned, preferred_element_type=F32)
    mixed += jnp.dot(weigh_low, returned, preferred_element_type=F32)
    scores = jnp.einsum("td,sd->ts", cotangent, returned, preferred_element_type=F32)
    scores = scores.reshape(tok_rows, expert_count, capacity)
    score_of = jnp.sum(jnp.where(slot_hot, scores, 0.0), axis=2)
    gate_grad = jnp.sum(jnp.where(pick_hot, score_of[:, None, :], 0.0), axis=2)
    x_grad = jnp.dot(select, back_grad, preferred_element_type=F32)
    swapped_in = jnp.concatenate([swapped_top, swapped_low], axis=0)
    grad_in = jnp.where(is_moved, swapped_in, grad_in)
    grad_out = jnp.concatenate([jnp.where(is_moved, theirs, own) for own, theirs in outs], axis=1)
    return (mixed.astype(BF16), x_grad.astype(BF16), gate_grad, grad_in[None], grad_out[None])


def solution(mesh):
    rows = P(("expert", "dp"), None)
    weights = P("expert", None, None)
    grads = P("expert", "dp", None)
    return jax.shard_map(
        shards,
        mesh=mesh,
        in_specs=(rows, rows, rows, rows, P(), weights, weights),
        out_specs=(rows, rows, rows, grads, grads),
        check_vma=False,
    )
```
